32 devices in a mesh: grp: 2 (over x), ra: 16 (over z, y, core).
Axes of the slice: x: 2, y: 2, z: 4, core: 2. Of those that a mesh axis runs over, the one named last changes fastest.
Arguments:
- observed_correlations: bfloat16 [1536, 351, 128], P(('grp', 'ra')), parts along dimension 0
- direction_per_batch: int32 [1536, 1], P(('grp', 'ra')), parts along dimension 0, may hold values from 0 to 15; in each aligned block of 48 rows (0 to 47, 48 to 95, ...) at most 6 rows name the same one
- receiver_pairings: int32 [702, 2], P('grp'), parts along dimension 0, may hold values from 0 to 26, as said below
- predicted_source_brightness: float32 [32, 16], P(('grp', 'ra')), parts along dimension 0, may hold values from 0.5 to 2
- starter_complex_factors: float32 [32, 2, 27, 16], P(('grp', 'ra')), parts along dimension 0, may hold values from 0.5 to 1.5
Outputs:
- solved_gains: float32 [32, 2, 27, 16], P(('grp', 'ra')), parts along dimension 0
The draws below stay inside these ranges and needn't reach their ends.
There are 2 independent parts, one for each index of `grp`. The reference program is written for one: setup_inputs(seed, part) draws one part's arguments, and reference() takes and returns one part's arrays. A program takes and returns all parts, laid end to end along the dimension named above; each array names one. Nothing has to cross between parts.
Inputs may be any that keep to these rules, and one draw needn't show every extreme that they name: `direction_per_batch`: among the 48 blocks held by one device, at most 6 name the same pointing. `receiver_pairings`: every unordered pair of two different antennas stands in exactly one row, in either order.
All inputs are finite; a program needn't handle non-finite values.
Results may differ from the reference program's by a relative error of at most 0.0003.
Values may be sent and summed in bfloat16 or wider, within the bound.
A program may use at most 128 MiB of HBM per device.

```python
import math
import jax
import jax.numpy as jnp
import numpy as np
from jax import lax

ANTENNA_COUNT = 27
BASE = 351
SPW = 16
CHS = 64
BLK_DEV = 48
ITERS = 2
NPT = 16
BLOCKS = 768
CAP = 6
N_RA = 16


def pair_table(key):
    upper_first, upper_second = np.triu_indices(ANTENNA_COUNT, 1)
    pairs = jnp.stack([jnp.asarray(upper_first, dtype=jnp.int32), jnp.asarray(upper_second, dtype=jnp.int32)], axis=1)
    order = jax.random.permutation(jax.random.fold_in(key, 11), BASE)
    pairs = pairs[order]
    flipped = jax.random.randint(jax.random.fold_in(key, 12), (BASE, 1), 0, 2)
    return jnp.where(flipped == 1, pairs[:, ::-1], pairs)


def draw_receiver_pairings(key, part):
    return pair_table(key)


def draw_observed_correlations(key, part):
    pairs = pair_table(key)
    key = jax.random.fold_in(key, 5)
    amp_key, mag_key, phase_key, real_key, imag_key = jax.random.split(key, 5)
    amplitude = jnp.exp(jax.random.uniform(amp_key, (BLOCKS, 1), jnp.float32, -0.6931, 0.6931))
    noise_re = 0.3 * jax.random.normal(real_key, (BLOCKS, BASE, CHS), jnp.float32)
    noise_im = 0.3 * jax.random.normal(imag_key, (BLOCKS, BASE, CHS), jnp.float32)
    magnitude = 1.0 + 0.5 * jax.random.uniform(mag_key, (BLOCKS, ANTENNA_COUNT), jnp.float32, -1.0, 1.0)
    phase = 0.6 * jax.random.uniform(phase_key, (BLOCKS, ANTENNA_COUNT), jnp.float32, -1.0, 1.0)
    true_re = magnitude * jnp.cos(phase)
    true_im = magnitude * jnp.sin(phase)
    leading_real = true_re[:, pairs[:, 0]]
    leading_imaginary = true_im[:, pairs[:, 0]]
    trailing_real = true_re[:, pairs[:, 1]]
    trailing_imaginary = true_im[:, pairs[:, 1]]
    signal_re = amplitude * (leading_real * trailing_real + leading_imaginary * trailing_imaginary)
    signal_im = amplitude * (leading_imaginary * trailing_real - leading_real * trailing_imaginary)
    data_re = signal_re[:, :, None] + noise_re
    data_im = signal_im[:, :, None] + noise_im
    return jnp.concatenate([data_re, data_im], axis=2).astype(jnp.bfloat16)


def block_scale(own_key, extent, pieces, smallest, high):
    gain = 1.0
    for position, parts in pieces:
        steps = jax.random.uniform(jax.random.fold_in(jax.random.fold_in(own_key, 6), position), (parts,), jnp.float32, smallest / len(pieces), high / len(pieces))
        gain = gain * jnp.repeat(jnp.exp(steps), extent[position] // parts).reshape((-1,) + (1,) * (len(extent) - 1 - position))
    return gain


def assign_block(own_key, own, number, rows, number_of, top, most, skew):
    sequence = jax.random.permutation(own_key, number_of)
    heavy_load, ordinary = shares(number_of, rows * top, most, skew, True), shares(number_of, rows * top, most, skew, False)
    places = jnp.arange(number_of)

    def named(sizes, rotation):
        used = int((sizes > 0).sum())
        fixed = max(1, used // 4)
        shifted = fixed + (places - fixed + rotation * (used - fixed)) % max(1, number_of - fixed)
        return jnp.zeros((number_of,), jnp.int32).at[sequence[jnp.where(places < fixed, places, shifted)]].set(jnp.asarray(sizes, jnp.int32))

    sizes = jnp.where(number % 4 == 0, named(heavy_load, number // 4), named(ordinary, number - number // 4 - 1))
    mixed = jax.random.permutation(jax.random.fold_in(own, 3), number_of)
    donor, sink = mixed[0:number_of // 2 * 2:2], mixed[1:number_of // 2 * 2:2]
    room = jnp.minimum(sizes[donor] - 1, most - sizes[sink]) // 2
    room = jnp.where((donor == sequence[0]) | (sink == sequence[0]) | (sizes[sink] == 0), 0, jnp.maximum(room, 0))
    shifted = jax.random.randint(jax.random.fold_in(own, 4), (number_of // 2,), 0, 1 << 20) % (room + 1)
    sizes = sizes.at[donor].add(-shifted).at[sink].add(shifted)
    items = jnp.searchsorted(jnp.cumsum(sizes), jnp.arange(rows * top), side="right").astype(jnp.int32)
    grid = items.reshape(top, rows).T
    grid = grid[jax.random.permutation(jax.random.fold_in(own, 1), rows)]
    rotation = jax.random.randint(jax.random.fold_in(own, 2), (rows, 1), 0, top)
    return jnp.take_along_axis(grid, (jnp.arange(top)[None, :] + rotation) % top, axis=1)


def shares(number_of, total, reach, lean, full):
    loads = [(1 << 20) // math.isqrt(grade ** lean) + 1 for grade in range(1, number_of + 1)]
    largest = reach if full else min(reach, max(-(-total // number_of), total * loads[0] // sum(loads)))
    least = 1 if total - largest >= number_of - 1 else 0
    given, rest = [largest] + [least] * (number_of - 1), total - largest - least * (number_of - 1)
    while rest > 0:
        movable = [i for i in range(1, number_of) if given[i] < largest] or [i for i in range(1, number_of) if given[i] < reach]
        mass, remaining = sum([loads[i] for i in movable]), rest
        for i in movable:
            more = min(reach - given[i], max(1, remaining * loads[i] // mass), rest)
            given[i] = given[i] + more
            rest = rest - more
    return np.array(given)


def setup_inputs(seed: int = 0, part: int = 0) -> dict:
    keys = jax.random.split(jax.random.key(seed), 6)
    own_keys = jax.random.split(jax.random.fold_in(keys[5], part), 6)
    observed_correlations = draw_observed_correlations(jax.random.fold_in(jax.random.fold_in(keys[5], part), 71), part)
    direction_per_batch_keys = jax.random.split(jax.random.fold_in(own_keys[1], 1), BLOCKS // BLK_DEV)
    direction_per_batch_turns = jax.random.permutation(jax.random.fold_in(own_keys[1], 3), BLOCKS // BLK_DEV)
    direction_per_batch = jax.vmap(lambda own, number: assign_block(jax.random.fold_in(own_keys[1], 2), own, number, BLK_DEV, N_RA, 1, CAP, 2))(direction_per_batch_keys, direction_per_batch_turns).reshape((BLOCKS, 1))
    receiver_pairings = draw_receiver_pairings(jax.random.fold_in(jax.random.fold_in(keys[5], part), 71), part)
    predicted_source_brightness = jnp.clip(jnp.exp(math.log(2.0) - 1.3862944 * jax.random.uniform(own_keys[3], (NPT, SPW), jnp.float32) ** block_scale(own_keys[3], (NPT, SPW), ((0, 16),), -0.2, 0.2)), 0.5, 2.0)
    starter_complex_factors = jnp.clip(0.5 + 1.0 * jax.random.uniform(own_keys[4], (NPT, 2, ANTENNA_COUNT, SPW), jnp.float32) ** block_scale(own_keys[4], (NPT, 2, ANTENNA_COUNT, SPW), ((0, 16),), -0.2, 0.2), 0.5, 1.5)
    return dict(observed_correlations=observed_correlations, direction_per_batch=direction_per_batch, receiver_pairings=receiver_pairings, predicted_source_brightness=predicted_source_brightness, starter_complex_factors=starter_complex_factors)


ROBUST = 0.5
COUPLING = 0.2
DAMPING = 100.0


def channel_sums(operands):
    blocks_data, pred_re, pred_im = operands
    middle = blocks_data.shape[-1] // 2
    data = blocks_data.astype(jnp.float32)
    data_re = data[..., :middle]
    data_im = data[..., middle:]
    resid_re = data_re - pred_re[..., None]
    resid_im = data_im - pred_im[..., None]
    weight = 1.0 / (1.0 + (resid_re * resid_re + resid_im * resid_im) / ROBUST)
    return (jnp.sum(weight, axis=-1), jnp.sum(weight * data_re, axis=-1), jnp.sum(weight * data_im, axis=-1))


def reference(observed_correlations, direction_per_batch, receiver_pairings, predicted_source_brightness, starter_complex_factors):
    total_blocks = observed_correlations.shape[0]
    target = direction_per_batch[:, 0]
    window_of = jnp.arange(total_blocks, dtype=jnp.int32) % SPW
    first_receiver = receiver_pairings[:, 0]
    second_receiver = receiver_pairings[:, 1]
    flux_rows = predicted_source_brightness[target, window_of][:, None]
    index_of_key = target * SPW + window_of
    leading_segment = (index_of_key[:, None] * ANTENNA_COUNT + first_receiver[None, :]).reshape(-1)
    trailing_segment = (index_of_key[:, None] * ANTENNA_COUNT + second_receiver[None, :]).reshape(-1)
    segments = NPT * SPW * ANTENNA_COUNT

    def gather_sum(to_first, to_second):
        summed = jax.ops.segment_sum(to_first.reshape(-1), leading_segment, segments) + jax.ops.segment_sum(to_second.reshape(-1), trailing_segment, segments)
        return jnp.transpose(summed.reshape(NPT, SPW, ANTENNA_COUNT), (0, 2, 1))

    current = starter_complex_factors
    for iteration in range(ITERS):
        selected_rows = current[target, :, :, window_of]
        leading_real = selected_rows[:, 0][:, first_receiver]
        leading_imaginary = selected_rows[:, 1][:, first_receiver]
        trailing_real = selected_rows[:, 0][:, second_receiver]
        trailing_imaginary = selected_rows[:, 1][:, second_receiver]
        pred_re = flux_rows * (leading_real * trailing_real + leading_imaginary * trailing_imaginary)
        pred_im = flux_rows * (leading_imaginary * trailing_real - leading_real * trailing_imaginary)
        shaped = observed_correlations.reshape(N_RA, BLK_DEV, BASE, 2 * CHS)
        totals = lax.map(channel_sums, (shaped, pred_re.reshape(N_RA, BLK_DEV, BASE), pred_im.reshape(N_RA, BLK_DEV, BASE)))
        weight_sum, weighted_re, weighted_im = [member.reshape(total_blocks, BASE) for member in totals]
        numer_re = gather_sum(flux_rows * (trailing_real * weighted_re - trailing_imaginary * weighted_im), flux_rows * (leading_real * weighted_re + leading_imaginary * weighted_im))
        numer_im = gather_sum(flux_rows * (trailing_real * weighted_im + trailing_imaginary * weighted_re), flux_rows * (leading_imaginary * weighted_re - leading_real * weighted_im))
        denom = gather_sum(flux_rows * flux_rows * (trailing_real * trailing_real + trailing_imaginary * trailing_imaginary) * weight_sum, flux_rows * flux_rows * (leading_real * leading_real + leading_imaginary * leading_imaginary) * weight_sum)
        own_re = (numer_re + DAMPING * current[:, 0]) / (denom + DAMPING)
        own_im = (numer_im + DAMPING * current[:, 1]) / (denom + DAMPING)
        own = jnp.stack([own_re, own_im], axis=1)
        current = (1.0 - 2.0 * COUPLING) * own + COUPLING * (jnp.roll(current, 1, axis=0) + jnp.roll(current, -1, axis=0))
    return current
```

```python
import functools

import jax
import jax.numpy as jnp
from jax import lax
from jax.experimental import pallas as pl
from jax.experimental.pallas import tpu as pltpu
from jax.sharding import PartitionSpec as P

ITERS = 2
ROBUST = 0.5
COUPLING = 0.2
DAMPING = 100.0
PRECISE = lax.Precision.HIGHEST
F32 = jnp.float32
BF16 = jnp.bfloat16

GROUP = 8
PART = 32
LANES = 128
PIECE = 32


def dot(a, b, ca=1, cb=0):
    return lax.dot_general(
        a, b, (((ca,), (cb,)), ((), ())), precision=PRECISE, preferred_element_type=F32
    )


def iota(shape, dim):
    return lax.broadcasted_iota(jnp.int32, shape, dim)


def kernel(
    n,
    x_ref,
    target_ref,
    pair_ref,
    flux_ref,
    start_ref,
    out_ref,
    raw,
    turned,
    tables,
    mine,
    slabs,
    partials,
    pred,
    sums,
    hot_rows,
    hot_cols,
    x_sem,
    send_sem,
    recv_sem,
):
    base, held, width = x_ref.shape
    rows = raw.shape[0]
    chunks = rows // GROUP
    lanes = GROUP * held
    half = width // 2
    antennas = start_ref.shape[3]
    windows = start_ref.shape[2]
    me = lax.axis_index("ra")

    loads = []
    for k, low in enumerate(range(0, base, PIECE)):
        size = min(PIECE, base - low)
        copy = pltpu.make_async_copy(
            x_ref.at[pl.ds(low, size)], raw.at[pl.ds(low, size)], x_sem.at[k]
        )
        copy.start()
        loads.append(copy)

    barrier = pltpu.get_barrier_semaphore()

    def greet(k, carry):
        pl.semaphore_signal(
            barrier,
            inc=1,
            device_id={"ra": lax.rem(me + k, n)},
            device_id_type=pl.DeviceIdType.MESH,
        )
        return carry

    lax.fori_loop(1, n, greet, 0)

    eye = iota((windows, windows), 0) == iota((windows, windows), 1)
    flux_col = jnp.sum(jnp.where(eye, flux_ref[...], 0.0), axis=1, keepdims=True)
    mine[...] = jnp.zeros_like(mine)
    mine[0, :, 0:antennas] = start_ref[0, 0]
    mine[0, :, PART : PART + antennas] = start_ref[0, 1]
    mine[0, :, 2 * PART : 2 * PART + 1] = flux_col

    pl.semaphore_wait(barrier, n - 1)

    def copy_to(phase, source, place, k):
        return pltpu.make_async_remote_copy(
            src_ref=source,
            dst_ref=place.at[me],
            send_sem=send_sem.at[phase],
            recv_sem=recv_sem.at[phase],
            device_id={"ra": lax.rem(me + k, n)},
            device_id_type=pl.DeviceIdType.MESH,
        )

    def send_gains(phase, it):
        def step(k, carry):
            copy_to(phase, mine.at[it], tables.at[it], k).start()
            return carry

        lax.fori_loop(1, n, step, 0)
        tables[it, me] = mine[it]

    def send_slabs(phase, it):
        def step(k, carry):
            copy_to(phase, slabs.at[it, lax.rem(me + k, n)], partials.at[it], k).start()
            return carry

        lax.fori_loop(1, n, step, 0)
        partials[it, me] = slabs[it, me]

    def finish(phase, place):
        whole = place.at[pl.ds(0, n - 1)]
        both = pltpu.make_async_remote_copy(
            src_ref=whole,
            dst_ref=whole,
            send_sem=send_sem.at[phase],
            recv_sem=recv_sem.at[phase],
            device_id={"ra": lax.rem(me + 1, n)},
            device_id_type=pl.DeviceIdType.MESH,
        )
        both.wait()

    send_gains(0, 0)

    names = iota((PART, base), 0)
    hot_cols[...] = jnp.zeros_like(hot_cols)
    hot_cols[:, 0:base] = jnp.where(names == pair_ref[0:1, :], 1.0, 0.0)
    hot_cols[:, rows : rows + base] = jnp.where(names == pair_ref[1:2, :], 1.0, 0.0)
    hot_rows[...] = hot_cols[...].T
    key = target_ref[...] * windows + lax.rem(iota((1, held), 1), windows)
    key_hot = jnp.where(iota((n * windows, held), 0) == key, 1.0, 0.0)
    gap = iota((held, lanes), 1) - iota((held, lanes), 0)
    spread = gap == 0
    for b in range(1, GROUP):
        spread = spread | (gap == b * held)
    spread = jnp.where(spread, 1.0, 0.0)
    offset = iota((GROUP, lanes), 1) - held * iota((GROUP, lanes), 0)
    own_lanes = (offset >= 0) & (offset < held)

    raw[pl.ds(base, rows - base)] = jnp.zeros((rows - base, held, width), BF16)

    def turn(k, carry):
        block = raw[pl.ds(k * GROUP, GROUP)].reshape(lanes, width)
        turned[k] = block.T.astype(F32)
        return carry

    for k, copy in enumerate(loads):
        copy.wait()
        lax.fori_loop(k * PIECE // GROUP, min((k + 1) * PIECE, rows) // GROUP, turn, 0)

    flux = None
    for it in range(ITERS):
        finish(2 * it, tables.at[it])
        table = tables[it].reshape(n * windows, LANES)
        chosen = dot(table, key_hot, 0, 0)
        if it == 0:
            flux = chosen[2 * PART : 2 * PART + 1]
        gain_re = dot(hot_rows[...], chosen[0:PART])
        gain_im = dot(hot_rows[...], chosen[PART : 2 * PART])
        g1r, g2r = gain_re[0:rows], gain_re[rows:]
        g1i, g2i = gain_im[0:rows], gain_im[rows:]
        pred[0:rows] = dot(flux * (g1r * g2r + g1i * g2i), spread)
        pred[rows:] = dot(flux * (g1i * g2r - g1r * g2i), spread)

        def work(k, carry):
            low = pl.multiple_of(k * GROUP, GROUP)
            p_re = jnp.sum(
                jnp.where(own_lanes, pred[pl.ds(low, GROUP)], 0.0), axis=0, keepdims=True
            )
            p_im = jnp.sum(
                jnp.where(own_lanes, pred[pl.ds(rows + low, GROUP)], 0.0), axis=0, keepdims=True
            )
            total = [jnp.zeros((8, lanes), F32) for _ in range(3)]
            for c in range(0, half, 8):
                re = turned[k, c : c + 8]
                im = turned[k, half + c : half + c + 8]
                d_re = re - p_re
                d_im = im - p_im
                weight = 1.0 / (d_re * d_re + d_im * d_im + ROBUST)
                total[0] = total[0] + weight
                total[1] = total[1] + weight * re
                total[2] = total[2] + weight * im
            for q in range(3):
                row = jnp.sum(total[q], axis=0, keepdims=True)
                sums[pl.ds(q * rows + low, GROUP)] = jnp.where(own_lanes, row, 0.0)
            return carry

        lax.fori_loop(0, chunks, work, 0)

        total = dot(sums[...], spread, 1, 1)
        w, wr, wi = total[0:rows], total[rows : 2 * rows], total[2 * rows :]
        scale = flux * ROBUST
        square = flux * scale
        terms = (
            (scale * (g2r * wr - g2i * wi), scale * (g1r * wr + g1i * wi)),
            (scale * (g2r * wi + g2i * wr), scale * (g1i * wr - g1r * wi)),
            (square * (g2r * g2r + g2i * g2i) * w, square * (g1r * g1r + g1i * g1i) * w),
        )
        normal = [dot(hot_cols[...], jnp.concatenate(pair, axis=0)) for pair in terms]
        normal.append(normal[2])
        slab = dot(key_hot, jnp.concatenate(normal, axis=0), 1, 1)
        slabs[it] = slab.reshape(n, windows, LANES)
        send_slabs(2 * it + 1, it)
        current = mine[it]
        near = tables[it, lax.rem(me + n - 1, n)] + tables[it, lax.rem(me + 1, n)]
        finish(2 * it + 1, partials.at[it])
        gathered = jnp.sum(partials[it], axis=0)
        denom = pltpu.roll(gathered, 2 * PART, 1)
        own = (gathered + DAMPING * current) / (denom + DAMPING)
        fresh = (1.0 - 2.0 * COUPLING) * own + COUPLING * near
        if it + 1 < ITERS:
            mine[it + 1] = jnp.where(iota(fresh.shape, 1) < 2 * PART, fresh, 0.0)
            send_gains(2 * it + 2, it + 1)
        else:
            out_ref[0, 0] = fresh[:, 0:antennas]
            out_ref[0, 1] = fresh[:, PART : PART + antennas]


def body(
    observed_correlations,
    direction_per_batch,
    receiver_pairings,
    predicted_source_brightness,
    starter_complex_factors,
):
    held, base, width = observed_correlations.shape
    antennas, windows = starter_complex_factors.shape[2:]
    n = lax.axis_size("ra")
    rows = -(-base // PIECE) * PIECE
    lanes = GROUP * held
    pieces = rows // PIECE
    vmem = pl.BlockSpec(memory_space=pltpu.VMEM)
    result = pl.pallas_call(
        functools.partial(kernel, n),
        out_shape=jax.ShapeDtypeStruct((1, 2, windows, antennas), F32),
        in_specs=[pl.BlockSpec(memory_space=pl.ANY)] + [vmem] * 4,
        out_specs=vmem,
        scratch_shapes=[
            pltpu.VMEM((rows, held, width), BF16),
            pltpu.VMEM((rows // GROUP, width, lanes), F32),
            pltpu.VMEM((ITERS, n, windows, LANES), F32),
            pltpu.VMEM((ITERS, windows, LANES), F32),
            pltpu.VMEM((ITERS, n, windows, LANES), F32),
            pltpu.VMEM((ITERS, n, windows, LANES), F32),
            pltpu.VMEM((2 * rows, lanes), F32),
            pltpu.VMEM((3 * rows, lanes), F32),
            pltpu.VMEM((2 * rows, PART), F32),
            pltpu.VMEM((PART, 2 * rows), F32),
            pltpu.SemaphoreType.DMA((pieces,)),
            pltpu.SemaphoreType.DMA((2 * ITERS,)),
            pltpu.SemaphoreType.DMA((2 * ITERS,)),
        ],
        compiler_params=pltpu.CompilerParams(
            collective_id=0, has_side_effects=True, vmem_limit_bytes=56 * 1024 * 1024
        ),
        cost_estimate=pl.CostEstimate(
            flops=60 * held * base * width, bytes_accessed=2 * held * base * width, transcendentals=0
        ),
    )(
        jnp.transpose(observed_correlations, (1, 0, 2)),
        direction_per_batch.T,
        receiver_pairings.T,
        predicted_source_brightness,
        jnp.transpose(starter_complex_factors, (0, 1, 3, 2)),
    )
    return jnp.transpose(result, (0, 1, 3, 2))


def solution(mesh):
    placed = (
        P(("grp", "ra"), None, None),
        P(("grp", "ra"), None),
        P("grp", None),
        P(("grp", "ra"), None),
        P(("grp", "ra"), None, None, None),
    )
    return jax.shard_map(
        body,
        mesh=mesh,
        in_specs=placed,
        out_specs=P(("grp", "ra"), None, None, None),
        check_vma=False,
    )
```

```python
import functools

import jax
import jax.numpy as jnp
from jax import lax
from jax.experimental import pallas as pl
from jax.experimental.pallas import tpu as pltpu
from jax.sharding import PartitionSpec as P

ITERS = 2
ROBUST = 0.5
COUPLING = 0.2
DAMPING = 100.0
F32 = jnp.float32
BF16 = jnp.bfloat16

GROUP = 8
PART = 32
LANES = 128
PIECE = 32


def dot(a, b, ca=1, cb=0):
    return lax.dot_general(a, b, (((ca,), (cb,)), ((), ())), preferred_element_type=F32)


def halves(x):
    high = x.astype(BF16)
    return high, (x - high.astype(F32)).astype(BF16)


def iota(shape, dim):
    return lax.broadcasted_iota(jnp.int32, shape, dim)


def kernel(
    n,
    x_ref,
    target_ref,
    pair_ref,
    flux_ref,
    start_ref,
    out_ref,
    raw,
    turned,
    tables,
    message,
    slabs,
    partials,
    state,
    pred,
    sums,
    hot_cols,
    to_gains,
    to_normals,
    key_hot,
    x_sem,
    send_sem,
    recv_sem,
):
    base, held, width = x_ref.shape
    rows = raw.shape[0]
    chunks = rows // GROUP
    places = sums.shape[1]
    lanes = GROUP * held
    span = hot_cols.shape[1] // 2
    half = width // 2
    antennas = start_ref.shape[3]
    windows = start_ref.shape[2]
    me = lax.axis_index("ra")

    loads = []
    for k, low in enumerate(range(0, base, PIECE)):
        size = min(PIECE, base - low)
        copy = pltpu.make_async_copy(
            x_ref.at[pl.ds(low, size)], raw.at[pl.ds(low, size)], x_sem.at[k]
        )
        copy.start()
        loads.append(copy)

    barrier = pltpu.get_barrier_semaphore()

    def greet(k, carry):
        pl.semaphore_signal(
            barrier,
            inc=1,
            device_id={"ra": lax.rem(me + k, n)},
            device_id_type=pl.DeviceIdType.MESH,
        )
        return carry

    lax.fori_loop(1, n, greet, 0)

    lane = iota((windows, LANES), 1)

    def pack(x):
        once = pltpu.roll(x, PART, 1)
        twice = pltpu.roll(x, 2 * PART, 1)
        wide = jnp.where(lane < PART, x, jnp.where(lane < 3 * PART, once, twice))
        high = wide.astype(BF16).astype(F32)
        is_high = (lane < PART) | ((lane >= 2 * PART) & (lane < 3 * PART))
        return jnp.where(is_high, high, wide - high).astype(BF16)

    def unpack(x):
        x = x + pltpu.roll(x, LANES - PART, 1)
        return jnp.where(lane < PART, x, pltpu.roll(x, LANES - PART, 1))

    eye = iota((windows, windows), 0) == iota((windows, windows), 1)
    flux_col = jnp.sum(jnp.where(eye, flux_ref[...], 0.0), axis=1, keepdims=True)
    state[...] = jnp.zeros_like(state)
    state[:, 0:antennas] = start_ref[0, 0]
    state[:, antennas : antennas + 1] = flux_col
    state[:, PART : PART + antennas] = start_ref[0, 1]
    current = state[...]
    message[0] = pack(current)

    names = iota((PART, base), 0)
    hot_cols[...] = jnp.zeros_like(hot_cols)
    hot_cols[:, 0:base] = jnp.where(names == pair_ref[0:1, :], 1.0, 0.0)
    hot_cols[:, span : span + base] = jnp.where(names == pair_ref[1:2, :], 1.0, 0.0)
    position = iota((1, GROUP * places), 1)
    part = jnp.zeros_like(position)
    for b in range(1, GROUP):
        part = part + jnp.where(position >= b * places, 1, 0)
    wanted = (position - places * part) * GROUP + part
    order = jnp.where(iota((span, GROUP * places), 0) == wanted, 1.0, 0.0).astype(BF16)
    hot_first = dot(hot_cols[:, 0:span].astype(BF16), order)
    hot_second = dot(hot_cols[:, span:].astype(BF16), order)
    for s, hot in enumerate((hot_first, hot_second)):
        twice = jnp.concatenate([hot, hot], axis=0).T
        to_gains[s * GROUP * places : (s + 1) * GROUP * places] = twice.astype(BF16)
    for b in range(GROUP):
        cut = slice(b * places, (b + 1) * places)
        pieces = [hot_first[:, cut]] * 2 + [hot_second[:, cut]] * 2
        to_normals[b * PART : (b + 1) * PART] = jnp.concatenate(pieces, axis=1).astype(BF16)
    key = target_ref[...] * windows + lax.rem(iota((1, held), 1), windows)
    keys = jnp.concatenate([key] * GROUP, axis=1)
    key_hot[...] = jnp.where(iota((n * windows, lanes), 0) == keys, 1.0, 0.0).astype(BF16)
    column = iota((1, lanes), 1)
    own_lanes = [(column >= b * held) & (column < (b + 1) * held) for b in range(GROUP)]

    def fold(x):
        size = x.shape[0] // GROUP
        out = x[0:size]
        for b in range(1, GROUP):
            out = jnp.where(own_lanes[b], x[b * size : (b + 1) * size], out)
        return out

    pl.semaphore_wait(barrier, n - 1)

    def copy_to(phase, source, place, k):
        return pltpu.make_async_remote_copy(
            src_ref=source,
            dst_ref=place.at[me],
            send_sem=send_sem.at[phase],
            recv_sem=recv_sem.at[phase],
            device_id={"ra": lax.rem(me + k, n)},
            device_id_type=pl.DeviceIdType.MESH,
        )

    def send_gains(phase, it):
        def step(k, carry):
            copy_to(phase, message.at[it], tables.at[it], k).start()
            return carry

        lax.fori_loop(1, n, step, 0)
        tables[it, me] = message[it]

    def send_slabs(phase, it):
        def step(k, carry):
            copy_to(phase, slabs.at[it, lax.rem(me + k, n)], partials.at[it], k).start()
            return carry

        lax.fori_loop(1, n, step, 0)
        partials[it, me] = slabs[it, me]

    def finish(phase, place):
        whole = place.at[pl.ds(0, n - 1)]
        both = pltpu.make_async_remote_copy(
            src_ref=whole,
            dst_ref=whole,
            send_sem=send_sem.at[phase],
            recv_sem=recv_sem.at[phase],
            device_id={"ra": lax.rem(me + 1, n)},
            device_id_type=pl.DeviceIdType.MESH,
        )
        both.wait()

    send_gains(0, 0)

    raw[pl.ds(base, rows - base)] = jnp.zeros((rows - base, held, width), BF16)
    for q in range(3):
        sums[q] = jnp.zeros((places, lanes), F32)

    def turn(k, carry):
        block = raw[pl.ds(k * GROUP, GROUP)].reshape(lanes, width)
        turned[k] = block.T.astype(F32)
        return carry

    for k, copy in enumerate(loads):
        copy.wait()
        lax.fori_loop(k * PIECE // GROUP, min((k + 1) * PIECE, rows) // GROUP, turn, 0)

    flux = None
    for it in range(ITERS):
        finish(2 * it, tables.at[it])
        chosen = dot(tables[it].reshape(n * windows, LANES), key_hot[...], 0, 0)
        if it == 0:
            flux = chosen[antennas : antennas + 1] + chosen[PART + antennas : PART + antennas + 1]
        gain_re = dot(to_gains[...], chosen[0 : 2 * PART].astype(BF16))
        gain_im = dot(to_gains[...], chosen[2 * PART :].astype(BF16))
        side = GROUP * places
        g1r, g2r = fold(gain_re[0:side]), fold(gain_re[side:])
        g1i, g2i = fold(gain_im[0:side]), fold(gain_im[side:])
        pred[0] = flux * (g1r * g2r + g1i * g2i)
        pred[1] = flux * (g1i * g2r - g1r * g2i)

        def work(k, carry):
            p_re = pred[0, pl.ds(k, 1)]
            p_im = pred[1, pl.ds(k, 1)]
            total = [jnp.zeros((8, lanes), F32) for _ in range(3)]
            for c in range(0, half, 8):
                re = turned[k, c : c + 8]
                im = turned[k, half + c : half + c + 8]
                d_re = re - p_re
                d_im = im - p_im
                weight = pl.reciprocal(d_re * d_re + d_im * d_im + ROBUST, approx=True)
                total[0] = total[0] + weight
                total[1] = total[1] + weight * re
                total[2] = total[2] + weight * im
            for q in range(3):
                sums[q, pl.ds(k, 1)] = jnp.sum(total[q], axis=0, keepdims=True)
            return carry

        lax.fori_loop(0, chunks, work, 0)

        w, wr, wi = sums[0], sums[1], sums[2]
        scale = flux * ROBUST
        square = flux * scale
        terms = (
            (scale * (g2r * wr - g2i * wi), scale * (g1r * wr + g1i * wi)),
            (scale * (g2r * wi + g2i * wr), scale * (g1i * wr - g1r * wi)),
            (square * (g2r * g2r + g2i * g2i) * w, square * (g1r * g1r + g1i * g1i) * w),
        )
        normal = []
        for one_first, one_second in terms:
            parts = jnp.concatenate(halves(one_first) + halves(one_second), axis=0)
            normal.append(fold(dot(to_normals[...], parts)))
        normal.append(normal[2])
        high, low = halves(jnp.concatenate(normal, axis=0))
        slab = dot(key_hot[...], high, 1, 1) + dot(key_hot[...], low, 1, 1)
        slabs[it] = slab.reshape(n, windows, LANES)
        send_slabs(2 * it + 1, it)
        before = tables[it, lax.rem(me + n - 1, n)].astype(F32)
        after = tables[it, lax.rem(me + 1, n)].astype(F32)
        near = unpack(before + after)
        finish(2 * it + 1, partials.at[it])
        gathered = jnp.sum(partials[it], axis=0)
        denom = pltpu.roll(gathered, 2 * PART, 1)
        own = (gathered + DAMPING * current) / (denom + DAMPING)
        fresh = (1.0 - 2.0 * COUPLING) * own + COUPLING * near
        if it + 1 < ITERS:
            current = jnp.where(lane < 2 * PART, fresh, 0.0)
            message[it + 1] = pack(current)
            send_gains(2 * it + 2, it + 1)
        else:
            out_ref[0, 0] = fresh[:, 0:antennas]
            out_ref[0, 1] = fresh[:, PART : PART + antennas]


def body(
    observed_correlations,
    direction_per_batch,
    receiver_pairings,
    predicted_source_brightness,
    starter_complex_factors,
):
    held, base, width = observed_correlations.shape
    antennas, windows = starter_complex_factors.shape[2:]
    n = lax.axis_size("ra")
    rows = -(-base // PIECE) * PIECE
    lanes = GROUP * held
    pieces = rows // PIECE
    places = -(-(rows // GROUP) // 16) * 16
    span = -(-rows // LANES) * LANES
    vmem = pl.BlockSpec(memory_space=pltpu.VMEM)
    result = pl.pallas_call(
        functools.partial(kernel, n),
        out_shape=jax.ShapeDtypeStruct((1, 2, windows, antennas), F32),
        in_specs=[pl.BlockSpec(memory_space=pl.ANY)] + [vmem] * 4,
        out_specs=vmem,
        scratch_shapes=[
            pltpu.VMEM((rows, held, width), BF16),
            pltpu.VMEM((rows // GROUP, width, lanes), F32),
            pltpu.VMEM((ITERS, n, windows, LANES), BF16),
            pltpu.VMEM((ITERS, windows, LANES), BF16),
            pltpu.VMEM((ITERS, n, windows, LANES), F32),
            pltpu.VMEM((ITERS, n, windows, LANES), F32),
            pltpu.VMEM((windows, LANES), F32),
            pltpu.VMEM((2, places, lanes), F32),
            pltpu.VMEM((3, places, lanes), F32),
            pltpu.VMEM((PART, 2 * span), F32),
            pltpu.VMEM((2 * GROUP * places, 2 * PART), BF16),
            pltpu.VMEM((GROUP * PART, 4 * places), BF16),
            pltpu.VMEM((n * windows, lanes), BF16),
            pltpu.SemaphoreType.DMA((pieces,)),
            pltpu.SemaphoreType.DMA((2 * ITERS,)),
            pltpu.SemaphoreType.DMA((2 * ITERS,)),
        ],
        compiler_params=pltpu.CompilerParams(
            collective_id=0, has_side_effects=True, vmem_limit_bytes=56 * 1024 * 1024
        ),
        cost_estimate=pl.CostEstimate(
            flops=60 * held * base * width, bytes_accessed=2 * held * base * width, transcendentals=0
        ),
    )(
        jnp.transpose(observed_correlations, (1, 0, 2)),
        direction_per_batch.T,
        receiver_pairings.T,
        predicted_source_brightness,
        jnp.transpose(starter_complex_factors, (0, 1, 3, 2)),
    )
    return jnp.transpose(result, (0, 1, 3, 2))


def solution(mesh):
    placed = (
        P(("grp", "ra"), None, None),
        P(("grp", "ra"), None),
        P("grp", None),
        P(("grp", "ra"), None),
        P(("grp", "ra"), None, None, None),
    )
    return jax.shard_map(
        body,
        mesh=mesh,
        in_specs=placed,
        out_specs=P(("grp", "ra"), None, None, None),
        check_vma=False,
    )
```

```python
import functools

import jax
import jax.numpy as jnp
from jax import lax
from jax.experimental import pallas as pl
from jax.experimental.pallas import tpu as pltpu
from jax.sharding import PartitionSpec as P

ITERS = 2
ROBUST = 0.5
COUPLING = 0.2
DAMPING = 100.0
F32 = jnp.float32
BF16 = jnp.bfloat16

GROUP = 8
PART = 32
LANES = 128
PIECE = 32
UNROLL = 4


def dot(a, b, ca=1, cb=0):
    return lax.dot_general(a, b, (((ca,), (cb,)), ((), ())), preferred_element_type=F32)


def halves(x):
    high = x.astype(BF16)
    return high, (x - high.astype(F32)).astype(BF16)


def iota(shape, dim):
    return lax.broadcasted_iota(jnp.int32, shape, dim)


def kernel(
    n,
    x_ref,
    target_ref,
    pair_ref,
    flux_ref,
    start_ref,
    out_ref,
    raw,
    turned,
    tables,
    message,
    slabs,
    partials,
    state,
    pred,
    sums,
    hot_cols,
    to_gains,
    to_normals,
    key_hot,
    x_sem,
    send_sem,
    recv_sem,
):
    base, held, width = x_ref.shape
    rows = raw.shape[0]
    chunks = rows // GROUP
    places = sums.shape[1]
    lanes = GROUP * held
    span = hot_cols.shape[1] // 2
    half = width // 2
    antennas = start_ref.shape[3]
    windows = start_ref.shape[2]
    kept = windows * 3 * PART // LANES
    rest = windows - kept
    me = lax.axis_index("ra")

    loads = []
    for k, low in enumerate(range(0, base, PIECE)):
        size = min(PIECE, base - low)
        copy = pltpu.make_async_copy(
            x_ref.at[pl.ds(low, size)], raw.at[pl.ds(low, size)], x_sem.at[k]
        )
        copy.start()
        loads.append(copy)

    barrier = pltpu.get_barrier_semaphore()

    def greet(k, carry):
        pl.semaphore_signal(
            barrier,
            inc=1,
            device_id={"ra": lax.rem(me + k, n)},
            device_id_type=pl.DeviceIdType.MESH,
        )
        return carry

    lax.fori_loop(1, n, greet, 0)

    lane = iota((windows, LANES), 1)

    def pack(x):
        once = pltpu.roll(x, PART, 1)
        twice = pltpu.roll(x, 2 * PART, 1)
        wide = jnp.where(lane < PART, x, jnp.where(lane < 3 * PART, once, twice))
        high = wide.astype(BF16).astype(F32)
        is_high = (lane < PART) | ((lane >= 2 * PART) & (lane < 3 * PART))
        return jnp.where(is_high, high, wide - high).astype(BF16)

    def unpack(x):
        x = x + pltpu.roll(x, LANES - PART, 1)
        return jnp.where(lane < PART, x, pltpu.roll(x, LANES - PART, 1))

    eye = iota((windows, windows), 0) == iota((windows, windows), 1)
    flux_col = jnp.sum(jnp.where(eye, flux_ref[...], 0.0), axis=1, keepdims=True)
    state[...] = jnp.zeros_like(state)
    state[:, 0:antennas] = start_ref[0, 0]
    state[:, antennas : antennas + 1] = flux_col
    state[:, PART : PART + antennas] = start_ref[0, 1]
    current = state[...]
    message[0] = pack(current)

    names = iota((PART, base), 0)
    hot_cols[...] = jnp.zeros_like(hot_cols)
    hot_cols[:, 0:base] = jnp.where(names == pair_ref[0:1, :], 1.0, 0.0)
    hot_cols[:, span : span + base] = jnp.where(names == pair_ref[1:2, :], 1.0, 0.0)
    position = iota((1, GROUP * places), 1)
    part = jnp.zeros_like(position)
    for b in range(1, GROUP):
        part = part + jnp.where(position >= b * places, 1, 0)
    wanted = (position - places * part) * GROUP + part
    order = jnp.where(iota((span, GROUP * places), 0) == wanted, 1.0, 0.0).astype(BF16)
    hot_first = dot(hot_cols[:, 0:span].astype(BF16), order)
    hot_second = dot(hot_cols[:, span:].astype(BF16), order)
    for s, hot in enumerate((hot_first, hot_second)):
        twice = jnp.concatenate([hot, hot], axis=0).T
        to_gains[s * GROUP * places : (s + 1) * GROUP * places] = twice.astype(BF16)
    for b in range(GROUP):
        cut = slice(b * places, (b + 1) * places)
        pieces = [hot_first[:, cut]] * 2 + [hot_second[:, cut]] * 2
        to_normals[b * PART : (b + 1) * PART] = jnp.concatenate(pieces, axis=1).astype(BF16)
    key = target_ref[...] * windows + lax.rem(iota((1, held), 1), windows)
    keys = jnp.concatenate([key] * GROUP, axis=1)
    key_hot[...] = jnp.where(iota((n * windows, lanes), 0) == keys, 1.0, 0.0).astype(BF16)
    column = iota((1, lanes), 1)
    own_lanes = [(column >= b * held) & (column < (b + 1) * held) for b in range(GROUP)]

    def fold(x):
        size = x.shape[0] // GROUP
        out = x[0:size]
        for b in range(1, GROUP):
            out = jnp.where(own_lanes[b], x[b * size : (b + 1) * size], out)
        return out

    pl.semaphore_wait(barrier, n - 1)

    def copy_to(phase, source, target, k):
        return pltpu.make_async_remote_copy(
            src_ref=source,
            dst_ref=target,
            send_sem=send_sem.at[phase],
            recv_sem=recv_sem.at[phase],
            device_id={"ra": lax.rem(me + k, n)},
            device_id_type=pl.DeviceIdType.MESH,
        )

    def send_gains(phase, it):
        def step(k, carry):
            copy_to(phase, message.at[it], tables.at[it, me], k).start()
            return carry

        lax.fori_loop(1, n, step, 0)
        tables[it, me] = message[it]

    def send_slabs(phase, it):
        def step(k, carry):
            source = slabs.at[it, lax.rem(me + k, n), pl.ds(0, kept)]
            copy_to(phase, source, partials.at[it, me, pl.ds(0, kept)], k).start()
            return carry

        lax.fori_loop(1, n, step, 0)
        partials[it, me, 0:kept] = slabs[it, me, 0:kept]

    def finish(phase, whole):
        both = pltpu.make_async_remote_copy(
            src_ref=whole,
            dst_ref=whole,
            send_sem=send_sem.at[phase],
            recv_sem=recv_sem.at[phase],
            device_id={"ra": lax.rem(me + 1, n)},
            device_id_type=pl.DeviceIdType.MESH,
        )
        both.wait()

    send_gains(0, 0)

    raw[pl.ds(base, rows - base)] = jnp.zeros((rows - base, held, width), BF16)
    for q in range(3):
        sums[q] = jnp.zeros((places, lanes), F32)

    def turn(k, carry):
        block = raw[pl.ds(k * GROUP, GROUP)].reshape(lanes, width)
        turned[k] = block.T.astype(F32)
        return carry

    for k, copy in enumerate(loads):
        copy.wait()
        lax.fori_loop(k * PIECE // GROUP, min((k + 1) * PIECE, rows) // GROUP, turn, 0)

    flux = None
    for it in range(ITERS):
        finish(2 * it, tables.at[it, pl.ds(0, n - 1)])
        chosen = dot(tables[it].reshape(n * windows, LANES), key_hot[...], 0, 0)
        if it == 0:
            flux = chosen[antennas : antennas + 1] + chosen[PART + antennas : PART + antennas + 1]
        gain_re = dot(to_gains[...], chosen[0 : 2 * PART].astype(BF16))
        gain_im = dot(to_gains[...], chosen[2 * PART :].astype(BF16))
        side = GROUP * places
        g1r, g2r = fold(gain_re[0:side]), fold(gain_re[side:])
        g1i, g2i = fold(gain_im[0:side]), fold(gain_im[side:])
        pred[0] = flux * (g1r * g2r + g1i * g2i)
        pred[1] = flux * (g1i * g2r - g1r * g2i)

        def work(k, carry):
            p_re = pred[0, pl.ds(k, 1)]
            p_im = pred[1, pl.ds(k, 1)]
            total = [jnp.zeros((8, lanes), F32) for _ in range(3)]
            for c in range(0, half, 8):
                re = turned[k, c : c + 8]
                im = turned[k, half + c : half + c + 8]
                d_re = re - p_re
                d_im = im - p_im
                weight = pl.reciprocal(d_re * d_re + d_im * d_im + ROBUST, approx=True)
                total[0] = total[0] + weight
                total[1] = total[1] + weight * re
                total[2] = total[2] + weight * im
            for q in range(3):
                sums[q, pl.ds(k, 1)] = jnp.sum(total[q], axis=0, keepdims=True)
            return carry

        lax.fori_loop(0, chunks, work, 0, unroll=UNROLL)

        w, wr, wi = sums[0], sums[1], sums[2]
        scale = flux * ROBUST
        square = flux * scale
        terms = (
            (scale * (g2r * wr - g2i * wi), scale * (g1r * wr + g1i * wi)),
            (scale * (g2r * wi + g2i * wr), scale * (g1i * wr - g1r * wi)),
            (square * (g2r * g2r + g2i * g2i) * w, square * (g1r * g1r + g1i * g1i) * w),
        )
        normal = []
        for one_first, one_second in terms:
            parts = jnp.concatenate(halves(one_first) + halves(one_second), axis=0)
            normal.append(fold(dot(to_normals[...], parts)))
        normal.append(jnp.zeros_like(normal[2]))
        high, low = halves(jnp.concatenate(normal, axis=0))
        slab = dot(key_hot[...], high, 1, 1) + dot(key_hot[...], low, 1, 1)
        slab = slab.reshape(n, windows, LANES)
        last = slab[:, kept:]
        fill = [pltpu.roll(last, LANES - (q + 1) * PART, 2) for q in range(3)]
        fill = jnp.concatenate(fill, axis=1)
        slabs[it, :, 0:kept] = jnp.where(
            iota((n, kept, LANES), 2) < 3 * PART, slab[:, 0:kept], fill
        )
        send_slabs(2 * it + 1, it)
        before = tables[it, lax.rem(me + n - 1, n)].astype(F32)
        after = tables[it, lax.rem(me + 1, n)].astype(F32)
        near = unpack(before + after)
        finish(2 * it + 1, partials.at[it, pl.ds(0, n - 1), pl.ds(0, kept)])
        gathered = jnp.sum(partials[it, :, 0:kept], axis=0)
        last = jnp.zeros((rest, LANES), F32)
        for q in range(3):
            moved = pltpu.roll(gathered[q * rest : (q + 1) * rest], (q + 1) * PART, 1)
            last = jnp.where(lane[0:rest] // PART == q, moved, last)
        gathered = jnp.concatenate([gathered, last], axis=0)
        denom = jnp.where(
            lane < PART,
            pltpu.roll(gathered, 2 * PART, 1),
            pltpu.roll(gathered, 3 * PART, 1),
        )
        own = (gathered + DAMPING * current) / (denom + DAMPING)
        fresh = (1.0 - 2.0 * COUPLING) * own + COUPLING * near
        if it + 1 < ITERS:
            current = jnp.where(lane < 2 * PART, fresh, 0.0)
            message[it + 1] = pack(current)
            send_gains(2 * it + 2, it + 1)
        else:
            out_ref[0, 0] = fresh[:, 0:antennas]
            out_ref[0, 1] = fresh[:, PART : PART + antennas]


def body(
    observed_correlations,
    direction_per_batch,
    receiver_pairings,
    predicted_source_brightness,
    starter_complex_factors,
):
    held, base, width = observed_correlations.shape
    antennas, windows = starter_complex_factors.shape[2:]
    n = lax.axis_size("ra")
    rows = -(-base // PIECE) * PIECE
    lanes = GROUP * held
    pieces = rows // PIECE
    places = -(-(rows // GROUP) // 16) * 16
    span = -(-rows // LANES) * LANES
    vmem = pl.BlockSpec(memory_space=pltpu.VMEM)
    result = pl.pallas_call(
        functools.partial(kernel, n),
        out_shape=jax.ShapeDtypeStruct((1, 2, windows, antennas), F32),
        in_specs=[pl.BlockSpec(memory_space=pl.ANY)] + [vmem] * 4,
        out_specs=vmem,
        scratch_shapes=[
            pltpu.VMEM((rows, held, width), BF16),
            pltpu.VMEM((rows // GROUP, width, lanes), F32),
            pltpu.VMEM((ITERS, n, windows, LANES), BF16),
            pltpu.VMEM((ITERS, windows, LANES), BF16),
            pltpu.VMEM((ITERS, n, windows, LANES), F32),
            pltpu.VMEM((ITERS, n, windows, LANES), F32),
            pltpu.VMEM((windows, LANES), F32),
            pltpu.VMEM((2, places, lanes), F32),
            pltpu.VMEM((3, places, lanes), F32),
            pltpu.VMEM((PART, 2 * span), F32),
            pltpu.VMEM((2 * GROUP * places, 2 * PART), BF16),
            pltpu.VMEM((GROUP * PART, 4 * places), BF16),
            pltpu.VMEM((n * windows, lanes), BF16),
            pltpu.SemaphoreType.DMA((pieces,)),
            pltpu.SemaphoreType.DMA((2 * ITERS,)),
            pltpu.SemaphoreType.DMA((2 * ITERS,)),
        ],
        compiler_params=pltpu.CompilerParams(
            collective_id=0, has_side_effects=True, vmem_limit_bytes=56 * 1024 * 1024
        ),
        cost_estimate=pl.CostEstimate(
            flops=60 * held * base * width, bytes_accessed=2 * held * base * width, transcendentals=0
        ),
    )(
        jnp.transpose(observed_correlations, (1, 0, 2)),
        direction_per_batch.T,
        receiver_pairings.T,
        predicted_source_brightness,
        jnp.transpose(starter_complex_factors, (0, 1, 3, 2)),
    )
    return jnp.transpose(result, (0, 1, 3, 2))


def solution(mesh):
    placed = (
        P(("grp", "ra"), None, None),
        P(("grp", "ra"), None),
        P("grp", None),
        P(("grp", "ra"), None),
        P(("grp", "ra"), None, None, None),
    )
    return jax.shard_map(
        body,
        mesh=mesh,
        in_specs=placed,
        out_specs=P(("grp", "ra"), None, None, None),
        check_vma=False,
    )
```

```python
import functools

import jax
import jax.numpy as jnp
from jax import lax
from jax.experimental import pallas as pl
from jax.experimental.pallas import tpu as pltpu
from jax.sharding import PartitionSpec as P

ITERS = 2
ROBUST = 0.5
COUPLING = 0.2
DAMPING = 100.0
F32 = jnp.float32
BF16 = jnp.bfloat16

GROUP = 8
PART = 32
LANES = 128
PIECE = 32
UNROLL = 4


def dot(a, b, ca=1, cb=0):
    return lax.dot_general(a, b, (((ca,), (cb,)), ((), ())), preferred_element_type=F32)


def halves(x):
    high = x.astype(BF16)
    return high, (x - high.astype(F32)).astype(BF16)


def iota(shape, dim):
    return lax.broadcasted_iota(jnp.int32, shape, dim)


def peer(me, n, k):
    odd = lax.rem(k, 2)
    away = lax.div(k + 1, 2)
    return lax.rem(me + odd * away + (1 - odd) * (n - away), n)


def kernel(
    n,
    x_ref,
    target_ref,
    pair_ref,
    flux_ref,
    start_ref,
    out_ref,
    raw,
    turned,
    tables,
    message,
    slabs,
    partials,
    state,
    pred,
    sums,
    hot_cols,
    to_gains,
    to_normals,
    key_hot,
    x_sem,
    send_sem,
    recv_sem,
):
    base, held, width = x_ref.shape
    rows = raw.shape[0]
    chunks = rows // GROUP
    places = sums.shape[1]
    lanes = GROUP * held
    span = hot_cols.shape[1] // 2
    half = width // 2
    antennas = start_ref.shape[3]
    windows = start_ref.shape[2]
    kept = windows * 3 * PART // LANES
    rest = windows - kept
    me = lax.axis_index("ra")

    loads = []
    for k, low in enumerate(range(0, base, PIECE)):
        size = min(PIECE, base - low)
        copy = pltpu.make_async_copy(
            x_ref.at[pl.ds(low, size)], raw.at[pl.ds(low, size)], x_sem.at[k]
        )
        copy.start()
        loads.append(copy)

    barrier = pltpu.get_barrier_semaphore()

    def greet(k, carry):
        pl.semaphore_signal(
            barrier,
            inc=1,
            device_id={"ra": peer(me, n, k)},
            device_id_type=pl.DeviceIdType.MESH,
        )
        return carry

    lax.fori_loop(1, n, greet, 0)

    lane = iota((windows, LANES), 1)

    def pack(x):
        once = pltpu.roll(x, PART, 1)
        twice = pltpu.roll(x, 2 * PART, 1)
        wide = jnp.where(lane < PART, x, jnp.where(lane < 3 * PART, once, twice))
        high = wide.astype(BF16).astype(F32)
        is_high = (lane < PART) | ((lane >= 2 * PART) & (lane < 3 * PART))
        return jnp.where(is_high, high, wide - high).astype(BF16)

    def unpack(x):
        x = x + pltpu.roll(x, LANES - PART, 1)
        return jnp.where(lane < PART, x, pltpu.roll(x, LANES - PART, 1))

    eye = iota((windows, windows), 0) == iota((windows, windows), 1)
    flux_col = jnp.sum(jnp.where(eye, flux_ref[...], 0.0), axis=1, keepdims=True)
    state[...] = jnp.zeros_like(state)
    state[:, 0:antennas] = start_ref[0, 0]
    state[:, antennas : antennas + 1] = flux_col
    state[:, PART : PART + antennas] = start_ref[0, 1]
    current = state[...]
    message[0] = pack(current)

    names = iota((PART, base), 0)
    hot_cols[...] = jnp.zeros_like(hot_cols)
    hot_cols[:, 0:base] = jnp.where(names == pair_ref[0:1, :], 1.0, 0.0)
    hot_cols[:, span : span + base] = jnp.where(names == pair_ref[1:2, :], 1.0, 0.0)
    position = iota((1, GROUP * places), 1)
    part = jnp.zeros_like(position)
    for b in range(1, GROUP):
        part = part + jnp.where(position >= b * places, 1, 0)
    wanted = (position - places * part) * GROUP + part
    order = jnp.where(iota((span, GROUP * places), 0) == wanted, 1.0, 0.0).astype(BF16)
    hot_first = dot(hot_cols[:, 0:span].astype(BF16), order)
    hot_second = dot(hot_cols[:, span:].astype(BF16), order)
    for s, hot in enumerate((hot_first, hot_second)):
        twice = jnp.concatenate([hot, hot], axis=0).T
        to_gains[s * GROUP * places : (s + 1) * GROUP * places] = twice.astype(BF16)
    for b in range(GROUP):
        cut = slice(b * places, (b + 1) * places)
        pieces = [hot_first[:, cut]] * 2 + [hot_second[:, cut]] * 2
        to_normals[b * PART : (b + 1) * PART] = jnp.concatenate(pieces, axis=1).astype(BF16)
    key = target_ref[...] * windows + lax.rem(iota((1, held), 1), windows)
    keys = jnp.concatenate([key] * GROUP, axis=1)
    key_hot[...] = jnp.where(iota((n * windows, lanes), 0) == keys, 1.0, 0.0).astype(BF16)
    column = iota((1, lanes), 1)
    own_lanes = [(column >= b * held) & (column < (b + 1) * held) for b in range(GROUP)]

    def fold(x):
        size = x.shape[0] // GROUP
        out = x[0:size]
        for b in range(1, GROUP):
            out = jnp.where(own_lanes[b], x[b * size : (b + 1) * size], out)
        return out

    pl.semaphore_wait(barrier, n - 1)

    def copy_to(phase, source, target, k):
        return pltpu.make_async_remote_copy(
            src_ref=source,
            dst_ref=target,
            send_sem=send_sem.at[phase],
            recv_sem=recv_sem.at[phase],
            device_id={"ra": peer(me, n, k)},
            device_id_type=pl.DeviceIdType.MESH,
        )

    def send_gains(phase, it):
        def step(k, carry):
            copy_to(phase, message.at[it], tables.at[it, me], k).start()
            return carry

        lax.fori_loop(1, n, step, 0)
        tables[it, me] = message[it]

    def send_slabs(phase, it):
        def step(k, carry):
            source = slabs.at[it, peer(me, n, k), pl.ds(0, kept)]
            copy_to(phase, source, partials.at[it, me, pl.ds(0, kept)], k).start()
            return carry

        lax.fori_loop(1, n, step, 0)
        partials[it, me, 0:kept] = slabs[it, me, 0:kept]

    def all_of(phase, whole):
        return pltpu.make_async_remote_copy(
            src_ref=whole,
            dst_ref=whole,
            send_sem=send_sem.at[phase],
            recv_sem=recv_sem.at[phase],
            device_id={"ra": lax.rem(me + 1, n)},
            device_id_type=pl.DeviceIdType.MESH,
        )

    send_gains(0, 0)

    raw[pl.ds(base, rows - base)] = jnp.zeros((rows - base, held, width), BF16)
    for q in range(3):
        sums[q] = jnp.zeros((places, lanes), F32)

    def turn(k, carry):
        block = raw[pl.ds(k * GROUP, GROUP)].reshape(lanes, width)
        turned[k] = block.T.astype(F32)
        return carry

    for k, copy in enumerate(loads):
        copy.wait()
        lax.fori_loop(k * PIECE // GROUP, min((k + 1) * PIECE, rows) // GROUP, turn, 0)

    flux = None
    sent = []
    for it in range(ITERS):
        gains_done = all_of(2 * it, tables.at[it, pl.ds(0, n - 1)])
        gains_done.wait_recv()
        chosen = dot(tables[it].reshape(n * windows, LANES), key_hot[...], 0, 0)
        if it == 0:
            flux = chosen[antennas : antennas + 1] + chosen[PART + antennas : PART + antennas + 1]
        gain_re = dot(to_gains[...], chosen[0 : 2 * PART].astype(BF16))
        gain_im = dot(to_gains[...], chosen[2 * PART :].astype(BF16))
        side = GROUP * places
        g1r, g2r = fold(gain_re[0:side]), fold(gain_re[side:])
        g1i, g2i = fold(gain_im[0:side]), fold(gain_im[side:])
        pred[0] = flux * (g1r * g2r + g1i * g2i)
        pred[1] = flux * (g1i * g2r - g1r * g2i)

        def work(k, carry):
            p_re = pred[0, pl.ds(k, 1)]
            p_im = pred[1, pl.ds(k, 1)]
            total = [jnp.zeros((8, lanes), F32) for _ in range(3)]
            for c in range(0, half, 8):
                re = turned[k, c : c + 8]
                im = turned[k, half + c : half + c + 8]
                d_re = re - p_re
                d_im = im - p_im
                weight = pl.reciprocal(d_re * d_re + d_im * d_im + ROBUST, approx=True)
                total[0] = total[0] + weight
                total[1] = total[1] + weight * re
                total[2] = total[2] + weight * im
            for q in range(3):
                sums[q, pl.ds(k, 1)] = jnp.sum(total[q], axis=0, keepdims=True)
            return carry

        lax.fori_loop(0, chunks, work, 0, unroll=UNROLL)

        w, wr, wi = sums[0], sums[1], sums[2]
        scale = flux * ROBUST
        square = flux * scale
        terms = (
            (scale * (g2r * wr - g2i * wi), scale * (g1r * wr + g1i * wi)),
            (scale * (g2r * wi + g2i * wr), scale * (g1i * wr - g1r * wi)),
            (square * (g2r * g2r + g2i * g2i) * w, square * (g1r * g1r + g1i * g1i) * w),
        )
        normal = []
        for one_first, one_second in terms:
            parts = jnp.concatenate(halves(one_first) + halves(one_second), axis=0)
            normal.append(fold(dot(to_normals[...], parts)))
        normal.append(jnp.zeros_like(normal[2]))
        high, low = halves(jnp.concatenate(normal, axis=0))
        slab = dot(key_hot[...], high, 1, 1) + dot(key_hot[...], low, 1, 1)
        slab = slab.reshape(n, windows, LANES)
        last = slab[:, kept:]
        fill = [pltpu.roll(last, LANES - (q + 1) * PART, 2) for q in range(3)]
        fill = jnp.concatenate(fill, axis=1)
        slabs[it, :, 0:kept] = jnp.where(
            iota((n, kept, LANES), 2) < 3 * PART, slab[:, 0:kept], fill
        )
        send_slabs(2 * it + 1, it)
        before = tables[it, lax.rem(me + n - 1, n)].astype(F32)
        after = tables[it, lax.rem(me + 1, n)].astype(F32)
        near = unpack(before + after)
        slabs_done = all_of(2 * it + 1, partials.at[it, pl.ds(0, n - 1), pl.ds(0, kept)])
        slabs_done.wait_recv()
        sent.extend([gains_done, slabs_done])
        gathered = jnp.sum(partials[it, :, 0:kept], axis=0)
        last = jnp.zeros((rest, LANES), F32)
        for q in range(3):
            moved = pltpu.roll(gathered[q * rest : (q + 1) * rest], (q + 1) * PART, 1)
            last = jnp.where(lane[0:rest] // PART == q, moved, last)
        gathered = jnp.concatenate([gathered, last], axis=0)
        denom = jnp.where(
            lane < PART,
            pltpu.roll(gathered, 2 * PART, 1),
            pltpu.roll(gathered, 3 * PART, 1),
        )
        own = (gathered + DAMPING * current) / (denom + DAMPING)
        fresh = (1.0 - 2.0 * COUPLING) * own + COUPLING * near
        if it + 1 < ITERS:
            current = jnp.where(lane < 2 * PART, fresh, 0.0)
            message[it + 1] = pack(current)
            send_gains(2 * it + 2, it + 1)
        else:
            out_ref[0, 0] = fresh[:, 0:antennas]
            out_ref[0, 1] = fresh[:, PART : PART + antennas]
    for copies in sent:
        copies.wait_send()


def body(
    observed_correlations,
    direction_per_batch,
    receiver_pairings,
    predicted_source_brightness,
    starter_complex_factors,
):
    held, base, width = observed_correlations.shape
    antennas, windows = starter_complex_factors.shape[2:]
    n = lax.axis_size("ra")
    rows = -(-base // PIECE) * PIECE
    lanes = GROUP * held
    pieces = rows // PIECE
    places = -(-(rows // GROUP) // 16) * 16
    span = -(-rows // LANES) * LANES
    vmem = pl.BlockSpec(memory_space=pltpu.VMEM)
    result = pl.pallas_call(
        functools.partial(kernel, n),
        out_shape=jax.ShapeDtypeStruct((1, 2, windows, antennas), F32),
        in_specs=[pl.BlockSpec(memory_space=pl.ANY)] + [vmem] * 4,
        out_specs=vmem,
        scratch_shapes=[
            pltpu.VMEM((rows, held, width), BF16),
            pltpu.VMEM((rows // GROUP, width, lanes), F32),
            pltpu.VMEM((ITERS, n, windows, LANES), BF16),
            pltpu.VMEM((ITERS, windows, LANES), BF16),
            pltpu.VMEM((ITERS, n, windows, LANES), F32),
            pltpu.VMEM((ITERS, n, windows, LANES), F32),
            pltpu.VMEM((windows, LANES), F32),
            pltpu.VMEM((2, places, lanes), F32),
            pltpu.VMEM((3, places, lanes), F32),
            pltpu.VMEM((PART, 2 * span), F32),
            pltpu.VMEM((2 * GROUP * places, 2 * PART), BF16),
            pltpu.VMEM((GROUP * PART, 4 * places), BF16),
            pltpu.VMEM((n * windows, lanes), BF16),
            pltpu.SemaphoreType.DMA((pieces,)),
            pltpu.SemaphoreType.DMA((2 * ITERS,)),
            pltpu.SemaphoreType.DMA((2 * ITERS,)),
        ],
        compiler_params=pltpu.CompilerParams(
            collective_id=0, has_side_effects=True, vmem_limit_bytes=56 * 1024 * 1024
        ),
        cost_estimate=pl.CostEstimate(
            flops=60 * held * base * width, bytes_accessed=2 * held * base * width, transcendentals=0
        ),
    )(
        jnp.transpose(observed_correlations, (1, 0, 2)),
        direction_per_batch.T,
        receiver_pairings.T,
        predicted_source_brightness,
        jnp.transpose(starter_complex_factors, (0, 1, 3, 2)),
    )
    return jnp.transpose(result, (0, 1, 3, 2))


def solution(mesh):
    placed = (
        P(("grp", "ra"), None, None),
        P(("grp", "ra"), None),
        P("grp", None),
        P(("grp", "ra"), None),
        P(("grp", "ra"), None, None, None),
    )
    return jax.shard_map(
        body,
        mesh=mesh,
        in_specs=placed,
        out_specs=P(("grp", "ra"), None, None, None),
        check_vma=False,
    )
```
